32 devices in a mesh: fsdp: 4 (over y, x), ed: 8 (over z, core).
Axes of the slice: x: 2, y: 2, z: 4, core: 2. Of those that a mesh axis runs over, the one named last changes fastest.
Arguments:
- tokens: bfloat16 [2304, 6144], P('ed', 'fsdp'), may hold values from -6 to 6
- expert_ids: int32 [2304, 2], P('ed'), may hold values from 0 to 7, all different within a row; in each aligned block of 288 rows (0 to 287, 288 to 575, ...) at most 81 rows name the same one
- route_weights: float32 [2304, 2], P('ed'), may hold values from 0.1 to 1
- w_gate: bfloat16 [1, 6144, 8192], P(None, 'fsdp', 'ed'), may hold values from -0.078125 to 0.078125
- w_up: bfloat16 [1, 6144, 8192], P(None, 'fsdp', 'ed'), may hold values from -0.078125 to 0.078125
- w_down: bfloat16 [1, 8192, 6144], P(None, 'ed', 'fsdp'), may hold values from -0.0625 to 0.0625
Outputs:
- mixed: bfloat16 [2304, 6144], P('ed', 'fsdp')
The draws below stay inside these ranges and needn't reach their ends.
Inputs may be any that keep to these rules, and one draw needn't show every extreme that they name: `expert_ids`: each row names two different experts. In each block of 288 rows that one index of ed holds, no expert is named by more than 81 rows, a bound that some block reaches.
All inputs are finite; a program needn't handle non-finite values.
Results may differ from the reference program's by a relative error of at most 0.025.
Values may be sent and summed in bfloat16 or wider, within the bound.
No kernel may reach another device: no remote copies, remote signals or barrier semaphores. Data moves between devices by JAX's collectives and lax.ppermute only.
A program may use at most 128 MiB of HBM per device.

```python
import math
import jax
import jax.numpy as jnp
import numpy as np
from jax import lax

D = 6144
EXPERTS = 8
FF = 8192
EW = 1
TOK_DEV = 288
CAP = 81
TOKENS = 2304
N_ED = 8


def steps_of(rng, extent, split, low, largest):
    level, own = 1.0, jax.random.fold_in(rng, 6)
    for dim, parts in split:
        draws = jnp.exp(jax.random.uniform(jax.random.fold_in(own, dim), (parts,), jnp.float32, low / len(split), largest / len(split)))
        level = level * jnp.repeat(draws, extent[dim] // parts).reshape([-1 if axis == dim else 1 for axis in range(len(extent))])
    return level


def assign_block(own_key, own, number, rows, amount, top, bound, lean):
    order = jax.random.permutation(own_key, amount)
    crowded, ordinary = portions_of(amount, rows * top, bound, lean, True), portions_of(amount, rows * top, bound, lean, False)
    places = jnp.arange(amount)

    def named(tallies, rotation):
        used = int((tallies > 0).sum())
        fixed = max(1, used // 4)
        moved = fixed + (places - fixed + rotation * (used - fixed)) % max(1, amount - fixed)
        return jnp.zeros((amount,), jnp.int32).at[order[jnp.where(places < fixed, places, moved)]].set(jnp.asarray(tallies, jnp.int32))

    tallies = jnp.where(number % 4 == 0, named(crowded, number // 4), named(ordinary, number - number // 4 - 1))
    mixed = jax.random.permutation(jax.random.fold_in(own, 3), amount)
    donor, receiver = mixed[0:amount // 2 * 2:2], mixed[1:amount // 2 * 2:2]
    slack = jnp.minimum(tallies[donor] - 1, bound - tallies[receiver]) // 2
    slack = jnp.where((donor == order[0]) | (receiver == order[0]) | (tallies[receiver] == 0), 0, jnp.maximum(slack, 0))
    moved = jax.random.randint(jax.random.fold_in(own, 4), (amount // 2,), 0, 1 << 20) % (slack + 1)
    tallies = tallies.at[donor].add(-moved).at[receiver].add(moved)
    items = jnp.searchsorted(jnp.cumsum(tallies), jnp.arange(rows * top), side="right").astype(jnp.int32)
    table = items.reshape(top, rows).T
    table = table[jax.random.permutation(jax.random.fold_in(own, 1), rows)]
    rotation = jax.random.randint(jax.random.fold_in(own, 2), (rows, 1), 0, top)
    return jnp.take_along_axis(table, (jnp.arange(top)[None, :] + rotation) % top, axis=1)


def portions_of(number_of, total, limit, slope, full):
    loads = [(1 << 20) // math.isqrt(standing ** slope) + 1 for standing in range(1, number_of + 1)]
    largest = limit if full else min(limit, max(-(-total // number_of), total * loads[0] // sum(loads)))
    least = 1 if total - largest >= number_of - 1 else 0
    given, surplus = [largest] + [least] * (number_of - 1), total - largest - least * (number_of - 1)
    while surplus > 0:
        movable = [i for i in range(1, number_of) if given[i] < largest] or [i for i in range(1, number_of) if given[i] < limit]
        pool, budget = sum([loads[i] for i in movable]), surplus
        for i in movable:
            more = min(limit - given[i], max(1, budget * loads[i] // pool), surplus)
            given[i] = given[i] + more
            surplus = surplus - more
    return np.array(given)


def scatter_about(rng, dims, width, most, split=(), kind=jnp.bfloat16):
    drawn = jax.random.normal(rng, dims, jnp.float32) * width
    if len(split) > 0:
        drawn = steps_of(rng, dims, split, -0.22, 0.18) * drawn
    return jnp.clip(drawn, min=-most, max=most).astype(kind)


def setup_inputs(seed: int = 0) -> dict:
    key_of = jax.random.split(jax.random.key(seed), 7)
    tokens = scatter_about(key_of[0], (TOKENS, D), 1.0, 6.0, ((0, 8), (1, 4)))
    expert_ids_keys = jax.random.split(jax.random.fold_in(key_of[1], 1), TOKENS // TOK_DEV)
    expert_ids_turns = jax.random.permutation(jax.random.fold_in(key_of[1], 3), TOKENS // TOK_DEV)
    expert_ids = jax.vmap(lambda own, number: assign_block(jax.random.fold_in(key_of[1], 2), own, number, TOK_DEV, EXPERTS, 2, CAP, 1))(expert_ids_keys, expert_ids_turns).reshape((TOKENS, 2))
    route_weights = jnp.clip(0.1 + 0.9 * jax.random.uniform(key_of[2], (TOKENS, 2), jnp.float32) ** steps_of(key_of[2], (TOKENS, 2), ((0, 8),), -0.2, 0.2), 0.1, 1.0)
    w_gate = scatter_about(key_of[3], (EW, D, FF), D ** -0.5, 0.078125, ((1, 4), (2, 8)))
    w_up = scatter_about(key_of[4], (EW, D, FF), D ** -0.5, 0.078125, ((1, 4), (2, 8)))
    w_down = scatter_about(key_of[5], (EW, FF, D), FF ** -0.5, 0.0625, ((1, 8), (2, 4)))
    return {"tokens": tokens, "expert_ids": expert_ids, "route_weights": route_weights, "w_gate": w_gate, "w_up": w_up, "w_down": w_down}


def slot_match(routes, window, capacity):
    window_ids = jnp.arange(window, dtype=jnp.int32)
    routed = jnp.any(routes[:, :, None, :] == window_ids[None, None, :, None], axis=3)
    position = jnp.cumsum(routed.astype(jnp.int32), axis=1) - 1
    slot_ids = jnp.arange(capacity, dtype=jnp.int32)
    hits = routed[:, :, :, None] & (position[:, :, :, None] == slot_ids[None, None, None, :])
    return hits.astype(jnp.int32)


def take_block(block_rows, row_list):
    return jnp.take(block_rows, row_list, axis=0)


def pick_rows(blocks, routes, window, capacity):
    match = slot_match(routes, window, capacity)
    row_numbers = jnp.arange(blocks.shape[1], dtype=jnp.int32)
    source_row = jnp.sum(match * row_numbers[None, :, None, None], axis=1).reshape(blocks.shape[0], window * capacity)
    filled = jnp.sum(match, axis=1).reshape(blocks.shape[0], window * capacity)
    picked = jax.vmap(take_block)(blocks, source_row)
    picked = jnp.where(filled[:, :, None] > 0, picked, jnp.zeros_like(picked))
    return picked.reshape(blocks.shape[0], window, capacity, blocks.shape[2])


def combine_matrix(routes, weights, window, capacity):
    match = slot_match(routes[None], window, capacity)[0]
    window_ids = jnp.arange(window, dtype=jnp.int32)
    per_expert = jnp.sum(jnp.where(routes[:, None, :] == window_ids[None, :, None], weights[:, None, :], jnp.zeros_like(weights[:, None, :])), axis=2)
    return (per_expert[:, :, None] * match.astype(weights.dtype)).reshape(routes.shape[0], window * capacity)


def reference(tokens, expert_ids, route_weights, w_gate, w_up, w_down):
    blocks = tokens.reshape(N_ED, TOK_DEV, D)
    route_blocks = expert_ids.reshape(N_ED, TOK_DEV, 2)
    weight_blocks = route_weights.reshape(N_ED, TOK_DEV, 2)
    selected = pick_rows(blocks, route_blocks, EW, CAP)
    selected = selected.transpose(1, 0, 2, 3).reshape(EW, N_ED * CAP, D)
    hidden_piece = FF // N_ED
    slot_total = N_ED * CAP

    def one_expert(operands):
        slot_rows_x, gate_weight, up_weight, down_weight = operands
        gate = jnp.dot(slot_rows_x, gate_weight, preferred_element_type=jnp.float32)
        up = jnp.dot(slot_rows_x, up_weight, preferred_element_type=jnp.float32)
        activation = (jax.nn.silu(gate) * up).astype(jnp.bfloat16)
        terms = jnp.einsum("rqk,qkd->qrd", activation.astype(jnp.float32).reshape(slot_total, N_ED, hidden_piece), down_weight.astype(jnp.float32).reshape(N_ED, hidden_piece, D))
        rounded = lax.optimization_barrier(terms.astype(jnp.bfloat16))
        return jnp.sum(rounded.astype(jnp.float32), axis=0)

    slot_out = lax.map(one_expert, (selected, w_gate, w_up, w_down))
    slot_out = slot_out.reshape(EW, N_ED, CAP, D).transpose(1, 0, 2, 3).reshape(N_ED, EW * CAP, D)
    matrices = jax.vmap(combine_matrix, in_axes=(0, 0, None, None))(route_blocks, weight_blocks, EW, CAP)
    mixed = jnp.einsum("stk,skd->std", matrices, slot_out, precision=lax.Precision.HIGHEST)
    return mixed.reshape(TOKENS, D).astype(jnp.bfloat16)
```

```python
import functools
import jax
import jax.numpy as jnp
from jax import lax
from jax.experimental import pallas as pl
from jax.experimental.pallas import tpu as pltpu
from jax.sharding import PartitionSpec as P

CAP = 81
LIMIT = 40 * 1024 * 1024


def params():
    return pltpu.CompilerParams(vmem_limit_bytes=LIMIT)


def vmem():
    return pl.BlockSpec(memory_space=pltpu.VMEM)


def one_hot_slots(ids_ref, slots, kind):
    ids = ids_ref[...]
    tokens = ids.shape[1]
    routed = jnp.max(jnp.where(ids == 0, 1.0, 0.0), axis=0, keepdims=True)
    below = lax.broadcasted_iota(jnp.int32, (tokens, tokens), 0) <= lax.broadcasted_iota(
        jnp.int32, (tokens, tokens), 1
    )
    place = jnp.dot(
        jnp.broadcast_to(routed, (8, tokens)).astype(jnp.bfloat16),
        jnp.where(below, 1.0, 0.0).astype(jnp.bfloat16),
        preferred_element_type=jnp.float32,
    )[0:1]
    place = jnp.where(routed > 0, place, 0.0)
    numbers = lax.broadcasted_iota(jnp.int32, (slots, tokens), 0).astype(jnp.float32) + 1.0
    return jnp.where(numbers == place, 1.0, 0.0).astype(kind)


def pick_kernel(ids_ref, tokens_ref, out_ref):
    hits = one_hot_slots(ids_ref, out_ref.shape[0], jnp.bfloat16)
    out_ref[...] = jnp.dot(hits, tokens_ref[...], preferred_element_type=jnp.float32).astype(
        out_ref.dtype
    )


def pick(ids, tokens, slots):
    return pl.pallas_call(
        pick_kernel,
        out_shape=jax.ShapeDtypeStruct((slots, tokens.shape[1]), tokens.dtype),
        in_specs=[vmem(), vmem()],
        out_specs=vmem(),
        compiler_params=params(),
        name="pick",
    )(ids, tokens)


def project_kernel(col, x_ref, *refs):
    weights, outs = refs[:4], refs[4:]
    step = pl.program_id(0)
    x = x_ref[...]
    quarter = weights[0].shape[1]
    for n, out in enumerate(outs):

        @pl.when(step == n)
        def _(out=out):
            for j, w in enumerate(weights):
                out[:, j * quarter : (j + 1) * quarter] = jnp.dot(
                    x, w[...], preferred_element_type=jnp.float32
                ).astype(out.dtype)


def project(columns, x, weights, order):
    rows, depth = x.shape
    parts = len(order)
    quarter = weights[0].shape[1] // parts
    kinds = [jnp.float32 if k == 0 else jnp.bfloat16 for k in order]
    if quarter % 128:
        outs = []
        for n, kind in enumerate(kinds):
            cut = [
                lax.dynamic_slice_in_dim(w, columns[n] * quarter, quarter, axis=1) for w in weights
            ]
            out = jnp.dot(x, jnp.concatenate(cut, axis=1), preferred_element_type=jnp.float32)
            outs.append(out.astype(kind))
        return outs
    whole = lambda n, col: (0, 0)
    grid_spec = pltpu.PrefetchScalarGridSpec(
        num_scalar_prefetch=1,
        grid=(parts,),
        in_specs=[pl.BlockSpec((rows, depth), whole)]
        + [pl.BlockSpec((depth, quarter), lambda n, col: (0, col[n]))] * 4,
        out_specs=[pl.BlockSpec((rows, 4 * quarter), whole)] * parts,
    )
    return pl.pallas_call(
        project_kernel,
        out_shape=[jax.ShapeDtypeStruct((rows, 4 * quarter), k) for k in kinds],
        grid_spec=grid_spec,
        compiler_params=params(),
        name="project",
    )(columns, x, *weights)


def down_kernel(col, *refs):
    parts = len(refs) - 4
    acts, (own, par, out_ref, total) = refs[:parts], refs[parts:]
    step = pl.program_id(0)
    quarter = own.shape[0]
    for n, act in enumerate(acts):

        @pl.when(step == n)
        def _(n=n, act=act):
            term = jnp.dot(act[:, :quarter], own[...], preferred_element_type=jnp.float32)
            term += jnp.dot(act[:, quarter:], par[...], preferred_element_type=jnp.float32)
            if n == 0:
                total[...] = term
            elif n < parts - 1:
                total[...] += term
            else:
                out_ref[...] = (total[...] + term).astype(out_ref.dtype)


def down(columns, acts, weights):
    parts = len(acts)
    rows = acts[0].shape[0]
    quarter, width = weights[0].shape[0] // parts, weights[0].shape[1]
    whole = lambda n, col: (0, 0)
    grid_spec = pltpu.PrefetchScalarGridSpec(
        num_scalar_prefetch=1,
        grid=(parts,),
        in_specs=[pl.BlockSpec((rows, 2 * quarter), whole)] * parts
        + [pl.BlockSpec((quarter, width), lambda n, col: (col[n], 0))] * 2,
        out_specs=pl.BlockSpec((rows, width), whole),
        scratch_shapes=[pltpu.VMEM((rows, width), jnp.float32)],
    )
    return pl.pallas_call(
        down_kernel,
        out_shape=jax.ShapeDtypeStruct((rows, width), jnp.bfloat16),
        grid_spec=grid_spec,
        compiler_params=params(),
        name="down",
    )(columns, *acts, *weights)


def combine_kernel(ids_ref, weights_ref, *refs):
    terms, out_ref = refs[:-1], refs[-1]
    slots = terms[0].shape[0]
    hits = one_hot_slots(ids_ref, slots, jnp.float32)
    scale = jnp.sum(jnp.where(ids_ref[...] == 0, weights_ref[...], 0.0), axis=0, keepdims=True)
    slot_out = terms[0][...].astype(jnp.float32)
    for term in terms[1:]:
        slot_out += term[...].astype(jnp.float32)
    out_ref[...] = lax.dot_general(
        hits * scale,
        slot_out,
        (((0,), (0,)), ((), ())),
        precision=lax.Precision.HIGHEST,
        preferred_element_type=jnp.float32,
    ).astype(out_ref.dtype)


def combine(ids, weights, terms):
    return pl.pallas_call(
        combine_kernel,
        out_shape=jax.ShapeDtypeStruct((ids.shape[1], terms[0].shape[1]), jnp.bfloat16),
        in_specs=[vmem()] * (2 + len(terms)),
        out_specs=vmem(),
        compiler_params=params(),
        name="combine",
    )(ids, weights, *terms)


def local(n_fsdp, n_ed, groups, tokens, expert_ids, route_weights, w_gate, w_up, w_down):
    slots = -(-CAP // 8) * 8
    swap = lambda v, axis, size, k: lax.ppermute(v, axis, [(i, i ^ k) for i in range(size)])
    partner = lambda v: swap(v, "ed", n_ed, 1)
    me = lax.axis_index("fsdp").astype(jnp.int32)
    order = list(range(n_fsdp))
    columns = me ^ jnp.array(order, jnp.int32)

    own = [w_gate[0], w_up[0], w_down[0]]
    other = [partner(w) for w in own]
    ids, scales = expert_ids.T, route_weights.T
    mine = pick(ids, tokens, slots)
    blocks = {0: mine}
    for s in range(1, n_ed // 2):
        blocks[s] = swap(mine, "ed", n_ed, 2 * s)

    sums = {}
    for group in groups:
        x = jnp.concatenate([blocks[s] for s in group], axis=0)
        parts = project(columns, x, [own[0], other[0], own[1], other[1]], order)
        total = parts[0]
        for k in range(1, n_fsdp):
            total = total + swap(parts[k], "fsdp", n_fsdp, k).astype(jnp.float32)
        half = total.shape[1] // 2
        act = (jax.nn.silu(total[:, :half]) * total[:, half:]).astype(jnp.bfloat16)
        acts = [act] + [swap(act, "fsdp", n_fsdp, k) for k in range(1, n_fsdp)]
        out = down(columns, acts, [own[2], other[2]])
        for i, s in enumerate(group):
            sums[s] = out[i * slots : (i + 1) * slots]
    terms = [sums[0]] + [swap(sums[s], "ed", n_ed, 2 * s) for s in range(1, n_ed // 2)]
    return combine(ids, scales, terms)


def solution(mesh):
    n_fsdp, n_ed = mesh.shape["fsdp"], mesh.shape["ed"]
    half = n_ed // 4
    groups = [list(range(half)), list(range(half, n_ed // 2))]
    return jax.shard_map(
        functools.partial(local, n_fsdp, n_ed, groups),
        mesh=mesh,
        in_specs=(
            P("ed", "fsdp"),
            P("ed", None),
            P("ed", None),
            P(None, "fsdp", "ed"),
            P(None, "fsdp", "ed"),
            P(None, "ed", "fsdp"),
        ),
        out_specs=P("ed", "fsdp"),
        check_vma=False,
    )
```

```python
import functools
import jax
import jax.numpy as jnp
from jax import lax
from jax.experimental import pallas as pl
from jax.experimental.pallas import tpu as pltpu
from jax.sharding import PartitionSpec as P

CAP = 81
LIMIT = 8 * 1024 * 1024
GROUPS = ((0, 1), (3,), (2,))
SEQ = ("P0", "P1", "A0", "P2", "A1", "D1", "A2", "D0", "D2")
WAIT = 1
ZORDER = (1, 3, 2)


def call(kernel, name, outs, args, after=(), flops=0):
    def body(*refs):
        kernel(*refs[len(after) :])

    return pl.pallas_call(
        body,
        out_shape=outs,
        in_specs=[pl.BlockSpec(memory_space=pl.ANY)] * len(after)
        + [pl.BlockSpec(memory_space=pltpu.VMEM)] * len(args),
        out_specs=[pl.BlockSpec(memory_space=pltpu.VMEM)] * len(outs),
        compiler_params=pltpu.CompilerParams(vmem_limit_bytes=LIMIT),
        cost_estimate=pl.CostEstimate(flops=flops, bytes_accessed=0, transcendentals=0),
        name=name,
    )(*after, *args)


def slot_hits(ids, slots):
    tokens = ids.shape[1]
    routed = jnp.max(jnp.where(ids == 0, 1.0, 0.0), axis=0, keepdims=True)
    upto = lax.broadcasted_iota(jnp.int32, (tokens, tokens), 0) <= lax.broadcasted_iota(
        jnp.int32, (tokens, tokens), 1
    )
    place = jnp.dot(
        jnp.broadcast_to(routed, (8, tokens)).astype(jnp.bfloat16),
        jnp.where(upto, 1.0, 0.0).astype(jnp.bfloat16),
        preferred_element_type=jnp.float32,
    )[0:1]
    place = jnp.where(routed > 0, place, 0.0)
    numbers = lax.broadcasted_iota(jnp.int32, (slots, tokens), 0).astype(jnp.float32) + 1.0
    return jnp.where(numbers == place, 1.0, 0.0)


def pick_kernel(ids_ref, tokens_ref, out_ref):
    hits = slot_hits(ids_ref[...], out_ref.shape[0])
    out_ref[...] = jnp.dot(
        hits.astype(jnp.bfloat16), tokens_ref[...], preferred_element_type=jnp.float32
    ).astype(out_ref.dtype)


def pick(ids, tokens, slots):
    outs = [jax.ShapeDtypeStruct((slots, tokens.shape[1]), tokens.dtype)]
    return call(pick_kernel, "pick", outs, [ids, tokens], flops=30000000000)[0]


def split(value):
    high = value.astype(jnp.bfloat16)
    return high, (value - high.astype(jnp.float32)).astype(jnp.bfloat16)


def back_kernel(ids_ref, scales_ref, high_ref, low_ref):
    ids = ids_ref[...]
    scale = jnp.sum(jnp.where(ids == 0, scales_ref[...], 0.0), axis=0, keepdims=True)
    high_ref[...], low_ref[...] = split((slot_hits(ids, high_ref.shape[1]) * scale).T)


def back(ids, scales, slots, after):
    outs = [jax.ShapeDtypeStruct((ids.shape[1], slots), jnp.bfloat16)] * 2
    return call(back_kernel, "back", outs, [ids, scales], after)


def project_kernel(parts, n_x, *refs):
    xs, weights, outs = refs[:n_x], refs[n_x:-parts], refs[-parts:]
    me = lax.axis_index("fsdp")
    x = xs[0][...] if n_x == 1 else jnp.concatenate([r[...] for r in xs], axis=0)
    quarter = weights[0].shape[1] // parts
    for k in [*range(parts - 1, 0, -1), 0]:
        cols = pl.ds(pl.multiple_of((me ^ k) * quarter, quarter), quarter)
        for j, w in enumerate(weights):
            outs[k][:, j * quarter : (j + 1) * quarter] = jnp.dot(
                x, w[:, cols], preferred_element_type=jnp.float32
            ).astype(outs[k].dtype)


def project(xs, weights, parts, after):
    rows, depth = len(xs) * xs[0].shape[0], xs[0].shape[1]
    quarter = weights[0].shape[1] // parts
    kinds = [jnp.float32] + [jnp.bfloat16] * (parts - 1)
    if quarter % 128:
        outs = []
        me = lax.axis_index("fsdp")
        x = jnp.concatenate(xs, axis=0)
        for k, kind in enumerate(kinds):
            cut = [
                lax.dynamic_slice_in_dim(w, (me ^ k) * quarter, quarter, axis=1) for w in weights
            ]
            out = jnp.dot(x, jnp.concatenate(cut, axis=1), preferred_element_type=jnp.float32)
            outs.append(out.astype(kind))
        return outs
    outs = [jax.ShapeDtypeStruct((rows, len(weights) * quarter), k) for k in kinds]
    kernel = functools.partial(project_kernel, parts, len(xs))
    flops = 2 * rows * depth * len(weights) * quarter * parts
    return call(kernel, "project", outs, [*xs, *weights], after, flops)


def act_kernel(*refs):
    parts, out_ref = refs[:-1], refs[-1]
    total = parts[0][...]
    for part in parts[1:]:
        total += part[...].astype(jnp.float32)
    half = total.shape[1] // 2
    gate, up = total[:, :half], total[:, half:]
    out_ref[...] = (gate / (1.0 + jnp.exp(-gate)) * up).astype(out_ref.dtype)


def activate(parts, after):
    rows, width = parts[0].shape
    outs = [jax.ShapeDtypeStruct((rows, width // 2), jnp.bfloat16)]
    return call(act_kernel, "act", outs, parts, after)[0]


def down_kernel(parts, n_w, *refs):
    acts, weights, outs = refs[:parts], refs[parts : parts + n_w], refs[parts + n_w :]
    me = lax.axis_index("fsdp")
    quarter = weights[0].shape[0] // parts
    rows = outs[0].shape[0]
    total = None
    for k, act in enumerate(acts):
        depth = pl.ds(pl.multiple_of((me ^ k) * quarter, quarter), quarter)
        for j, w in enumerate(weights):
            term = jnp.dot(
                act[:, j * quarter : (j + 1) * quarter],
                w[depth, :],
                preferred_element_type=jnp.float32,
            )
            total = term if total is None else total + term
    for i, out in enumerate(outs):
        out[...] = total[i * rows : (i + 1) * rows].astype(out.dtype)


def down(acts, weights, blocks, after):
    parts, rows, width = len(acts), acts[0].shape[0], weights[0].shape[1]
    outs = [jax.ShapeDtypeStruct((rows // blocks, width), jnp.bfloat16)] * blocks
    kernel = functools.partial(down_kernel, parts, len(weights))
    flops = 2 * rows * weights[0].shape[0] * len(weights) * width
    return call(kernel, "down", outs, [*acts, *weights], after, flops)


def combine_kernel(back_high, back_low, *refs):
    terms, out_ref = refs[:-1], refs[-1]
    slot_out = terms[0][...].astype(jnp.float32)
    for term in terms[1:]:
        slot_out += term[...].astype(jnp.float32)
    high, low = split(slot_out)
    total = jnp.dot(back_low[...], high, preferred_element_type=jnp.float32)
    total += jnp.dot(back_high[...], low, preferred_element_type=jnp.float32)
    total += jnp.dot(back_high[...], high, preferred_element_type=jnp.float32)
    out_ref[...] = total.astype(out_ref.dtype)


def combine(backs, terms):
    outs = [jax.ShapeDtypeStruct((backs[0].shape[0], terms[0].shape[1]), jnp.bfloat16)]
    return call(combine_kernel, "combine", outs, [*backs, *terms])[0]


def local(n_fsdp, n_ed, groups, zorder, seq, tokens, expert_ids, route_weights, w_gate, w_up, w_down):
    slots = -(-CAP // 8) * 8
    swap = lambda v, axis, size, k: lax.ppermute(v, axis, [(i, i ^ k) for i in range(size)])
    partner = lambda v: swap(v, "ed", n_ed, 1)
    along = lambda v, s: swap(v, "ed", n_ed, 2 * s)
    across = lambda v, k: swap(v, "fsdp", n_fsdp, k)
    own = [w_gate[0], w_up[0], w_down[0]]
    other = [partner(w) for w in own]
    mine = pick(expert_ids.T, tokens, slots)
    backs = back(expert_ids.T, route_weights.T, slots, (mine,))
    blocks = {0: mine}
    for s in zorder:
        blocks[s] = along(mine, s)

    parts, acts, terms, last = {}, {}, [], (backs[0],)
    for word in seq:
        op, g = word[0], int(word[1:])
        group = groups[g]
        if op == "P":
            xs = [blocks[s] for s in group]
            weights = [own[0], other[0], own[1], other[1]]
            out = project(xs, weights, n_fsdp, (*last, other[2]) if g == WAIT else last)
            parts[g] = [out[0]] + [across(out[k], k) for k in range(n_fsdp - 1, 0, -1)][::-1]
            last = (out[0],)
        elif op == "A":
            act = activate(parts[g], last)
            acts[g] = [act] + [across(act, k) for k in range(n_fsdp - 1, 0, -1)][::-1]
            last = (act,)
        else:
            outs = down(acts[g], [own[2], other[2]], len(group), last)
            last = (outs[0],)
            terms += [out if s == 0 else along(out, s) for s, out in zip(group, outs)]
    return combine(backs, terms)


def plan(n_ed):
    if n_ed == 8:
        return GROUPS, ZORDER, SEQ
    half = n_ed // 4
    groups = (tuple(range(half)), tuple(range(half, n_ed // 2)))
    return groups, tuple(range(1, n_ed // 2)), ("P0", "P1", "A0", "A1", "D0", "D1")


def solution(mesh):
    n_fsdp, n_ed = mesh.shape["fsdp"], mesh.shape["ed"]
    return jax.shard_map(
        functools.partial(local, n_fsdp, n_ed, *plan(n_ed)),
        mesh=mesh,
        in_specs=(
            P("ed", "fsdp"),
            P("ed", None),
            P("ed", None),
            P(None, "fsdp", "ed"),
            P(None, "fsdp", "ed"),
            P(None, "ed", "fsdp"),
        ),
        out_specs=P("ed", "fsdp"),
        check_vma=False,
    )
```

```python
import functools
import jax
import jax.numpy as jnp
from jax import lax
from jax.experimental import pallas as pl
from jax.experimental.pallas import tpu as pltpu
from jax.sharding import PartitionSpec as P

CAP = 81
LIMIT = 8 * 1024 * 1024
GROUPS = ((0, 1), (3,), (2,))
SEQ = ("P0", "P1", "A0", "P2", "A1", "D1", "A2", "D0", "D2")
WAIT = 1
ZORDER = (1, 3, 2)


def call(kernel, name, outs, args, after=(), flops=0, scratch=()):
    def body(*refs):
        kernel(*refs[len(after) :])

    return pl.pallas_call(
        body,
        out_shape=outs,
        in_specs=[pl.BlockSpec(memory_space=pl.ANY)] * len(after)
        + [pl.BlockSpec(memory_space=pltpu.VMEM)] * len(args),
        out_specs=[pl.BlockSpec(memory_space=pltpu.VMEM)] * len(outs),
        scratch_shapes=list(scratch),
        compiler_params=pltpu.CompilerParams(vmem_limit_bytes=LIMIT),
        cost_estimate=pl.CostEstimate(flops=flops, bytes_accessed=0, transcendentals=0),
        name=name,
    )(*after, *args)


def slot_hits(ids, slots):
    tokens = ids.shape[1]
    routed = jnp.max(jnp.where(ids == 0, 1.0, 0.0), axis=0, keepdims=True)
    upto = lax.broadcasted_iota(jnp.int32, (tokens, tokens), 0) <= lax.broadcasted_iota(
        jnp.int32, (tokens, tokens), 1
    )
    place = jnp.dot(
        jnp.broadcast_to(routed, (8, tokens)).astype(jnp.bfloat16),
        jnp.where(upto, 1.0, 0.0).astype(jnp.bfloat16),
        preferred_element_type=jnp.float32,
    )[0:1]
    place = jnp.where(routed > 0, place, 0.0)
    numbers = lax.broadcasted_iota(jnp.int32, (slots, tokens), 0).astype(jnp.float32) + 1.0
    return jnp.where(numbers == place, 1.0, 0.0)


def pick_kernel(ids_ref, tokens_ref, out_ref):
    hits = slot_hits(ids_ref[...], out_ref.shape[0])
    out_ref[...] = jnp.dot(
        hits.astype(jnp.bfloat16), tokens_ref[...], preferred_element_type=jnp.float32
    ).astype(out_ref.dtype)


def pick(ids, tokens, slots):
    outs = [jax.ShapeDtypeStruct((slots, tokens.shape[1]), tokens.dtype)]
    return call(pick_kernel, "pick", outs, [ids, tokens], flops=30000000000)[0]


def split(value):
    high = value.astype(jnp.bfloat16)
    return high, (value - high.astype(jnp.float32)).astype(jnp.bfloat16)


def back_kernel(ids_ref, scales_ref, high_ref, low_ref):
    ids = ids_ref[...]
    scale = jnp.sum(jnp.where(ids == 0, scales_ref[...], 0.0), axis=0, keepdims=True)
    high_ref[...], low_ref[...] = split((slot_hits(ids, high_ref.shape[1]) * scale).T)


def back(ids, scales, slots, after):
    outs = [jax.ShapeDtypeStruct((ids.shape[1], slots), jnp.bfloat16)] * 2
    return call(back_kernel, "back", outs, [ids, scales], after)


def project_kernel(parts, n_x, *refs):
    xs, weights, outs = refs[:n_x], refs[n_x:-parts], refs[-parts:]
    me = lax.axis_index("fsdp")
    x = xs[0][...] if n_x == 1 else jnp.concatenate([r[...] for r in xs], axis=0)
    quarter = weights[0].shape[1] // parts
    for k in [*range(parts - 1, 0, -1), 0]:
        cols = pl.ds(pl.multiple_of((me ^ k) * quarter, quarter), quarter)
        for j, w in enumerate(weights):
            outs[k][:, j * quarter : (j + 1) * quarter] = jnp.dot(
                x, w[:, cols], preferred_element_type=jnp.float32
            ).astype(outs[k].dtype)


def project(xs, weights, parts, after):
    rows, depth = len(xs) * xs[0].shape[0], xs[0].shape[1]
    quarter = weights[0].shape[1] // parts
    kinds = [jnp.float32] + [jnp.bfloat16] * (parts - 1)
    if quarter % 128:
        outs = []
        me = lax.axis_index("fsdp")
        x = jnp.concatenate(xs, axis=0)
        for k, kind in enumerate(kinds):
            cut = [
                lax.dynamic_slice_in_dim(w, (me ^ k) * quarter, quarter, axis=1) for w in weights
            ]
            out = jnp.dot(x, jnp.concatenate(cut, axis=1), preferred_element_type=jnp.float32)
            outs.append(out.astype(kind))
        return outs
    outs = [jax.ShapeDtypeStruct((rows, len(weights) * quarter), k) for k in kinds]
    kernel = functools.partial(project_kernel, parts, len(xs))
    flops = 2 * rows * depth * len(weights) * quarter * parts
    return call(kernel, "project", outs, [*xs, *weights], after, flops)


def act_kernel(*refs):
    parts, out_ref = refs[:-1], refs[-1]
    total = parts[0][...]
    for part in parts[1:]:
        total += part[...].astype(jnp.float32)
    half = total.shape[1] // 2
    gate, up = total[:, :half], total[:, half:]
    out_ref[...] = (gate / (1.0 + jnp.exp(-gate)) * up).astype(out_ref.dtype)


def activate(parts, after):
    rows, width = parts[0].shape
    outs = [jax.ShapeDtypeStruct((rows, width // 2), jnp.bfloat16)]
    return call(act_kernel, "act", outs, parts, after)[0]


def down_kernel(parts, n_w, *refs):
    acts, weights, outs = refs[:parts], refs[parts : parts + n_w], refs[parts + n_w :]
    me = lax.axis_index("fsdp")
    quarter = weights[0].shape[0] // parts
    rows = outs[0].shape[0]
    total = None
    for k, act in enumerate(acts):
        depth = pl.ds(pl.multiple_of((me ^ k) * quarter, quarter), quarter)
        for j, w in enumerate(weights):
            term = jnp.dot(
                act[:, j * quarter : (j + 1) * quarter],
                w[depth, :],
                preferred_element_type=jnp.float32,
            )
            total = term if total is None else total + term
    for i, out in enumerate(outs):
        out[...] = total[i * rows : (i + 1) * rows].astype(out.dtype)


def down(acts, weights, blocks, after):
    parts, rows, width = len(acts), acts[0].shape[0], weights[0].shape[1]
    outs = [jax.ShapeDtypeStruct((rows // blocks, width), jnp.bfloat16)] * blocks
    kernel = functools.partial(down_kernel, parts, len(weights))
    flops = 2 * rows * weights[0].shape[0] * len(weights) * width
    return call(kernel, "down", outs, [*acts, *weights], after, flops)


def combine_kernel(back_high, back_low, *refs):
    terms, out_ref = refs[:-1], refs[-1]
    slot_out = terms[0][...].astype(jnp.float32)
    for term in terms[1:]:
        slot_out += term[...].astype(jnp.float32)
    high, low = split(slot_out)
    total = jnp.dot(back_low[...], high, preferred_element_type=jnp.float32)
    total += jnp.dot(back_high[...], low, preferred_element_type=jnp.float32)
    total += jnp.dot(back_high[...], high, preferred_element_type=jnp.float32)
    out_ref[...] = total.astype(out_ref.dtype)


def combine(backs, terms):
    outs = [jax.ShapeDtypeStruct((backs[0].shape[0], terms[0].shape[1]), jnp.bfloat16)]
    return call(combine_kernel, "combine", outs, [*backs, *terms])[0]


def lead_of(count):
    lead = count // 16 * 16
    return lead, count - lead


def packed_rows(blocks, columns):
    return blocks * CAP * columns // 128


def to_rows(value):
    return [value[:, 128 * j : 128 * (j + 1)] for j in range(value.shape[1] // 128)]


def pack(out_ref, value, blocks, first=0, of=None):
    lead, rest = lead_of(CAP)
    of = blocks if of is None else of
    wide = value.shape[1] // 128
    for n in range(blocks):
        for j in range(wide):
            out_ref[(n * wide + j) * lead : (n * wide + j + 1) * lead, :] = value[
                (first + n) * lead : (first + n + 1) * lead, 128 * j : 128 * (j + 1)
            ].astype(out_ref.dtype)
    others = []
    for n in range(blocks):
        for i in range(rest):
            row = of * lead + (first + n) * rest + i
            others += to_rows(value[row : row + 1])
    if others:
        start = blocks * wide * lead
        out_ref[start : start + len(others), :] = jnp.concatenate(others, axis=0).astype(out_ref.dtype)


def unpack(refs, held, at=0):
    lead, rest = lead_of(CAP)
    blocks = sum(n for _, n in refs)
    others, done = [], 0
    for ref, count in refs:
        wide = ref.shape[0] // (count * CAP)
        for n in range(count):
            for j in range(wide):
                held[
                    (done + n) * lead : (done + n + 1) * lead, at + 128 * j : at + 128 * (j + 1)
                ] = ref[(n * wide + j) * lead : (n * wide + j + 1) * lead, :]
        if rest:
            last = ref[count * wide * lead : count * wide * (lead + rest), :].astype(jnp.float32)
            for n in range(count * rest):
                rows = [last[n * wide + j : n * wide + j + 1] for j in range(wide)]
                others.append(jnp.concatenate(rows, axis=1))
        done += count
    room = held.shape[0] - blocks * lead
    if room:
        width = 128 * wide
        others.append(jnp.zeros((room - len(others), width), jnp.float32))
        held[blocks * lead :, at : at + width] = jnp.concatenate(others, axis=0).astype(held.dtype)


def room_for(blocks):
    lead, rest = lead_of(CAP)
    return blocks * lead + -(-blocks * rest // 16) * 16


def pick_packed_kernel(ids_ref, tokens_ref, out_ref):
    hits = slot_hits(ids_ref[...], -(-CAP // 8) * 8).astype(jnp.bfloat16)
    pack(out_ref, jnp.dot(hits, tokens_ref[...], preferred_element_type=jnp.float32), 1)


def pick_packed(ids, tokens):
    outs = [jax.ShapeDtypeStruct((packed_rows(1, tokens.shape[1]), 128), tokens.dtype)]
    return call(pick_packed_kernel, "pick", outs, [ids, tokens], flops=30000000000)[0]


def project_packed_kernel(parts, n_x, *refs):
    xs, weights, outs, held = refs[:n_x], refs[n_x:-parts - 1], refs[-parts - 1 : -1], refs[-1]
    me = lax.axis_index("fsdp")
    unpack([(x, 1) for x in xs], held)
    x = held[...]
    quarter = weights[0].shape[1] // parts
    for k in [*range(parts - 1, 0, -1), 0]:
        cols = pl.ds(pl.multiple_of((me ^ k) * quarter, quarter), quarter)
        value = [jnp.dot(x, w[:, cols], preferred_element_type=jnp.float32) for w in weights]
        pack(outs[k], jnp.concatenate(value, axis=1), n_x)


def project_packed(xs, weights, parts, after):
    depth, width = weights[0].shape
    quarter = width // parts
    rows = room_for(len(xs))
    kinds = [jnp.float32] + [jnp.bfloat16] * (parts - 1)
    size = (packed_rows(len(xs), len(weights) * quarter), 128)
    outs = [jax.ShapeDtypeStruct(size, kind) for kind in kinds]
    kernel = functools.partial(project_packed_kernel, parts, len(xs))
    flops = 2 * rows * depth * len(weights) * width
    scratch = [pltpu.VMEM((rows, depth), xs[0].dtype)]
    return call(kernel, "project", outs, [*xs, *weights], after, flops, scratch)


def act_packed_kernel(blocks, *refs):
    parts, out_ref = refs[:-1], refs[-1]
    total = parts[0][...]
    for part in parts[1:]:
        total += part[...].astype(jnp.float32)
    lead, rest = lead_of(CAP)
    wide = total.shape[0] // (blocks * CAP)
    half = wide // 2

    def act(start, rows):
        gate, up = total[start : start + rows], total[start + rows : start + 2 * rows]
        return gate / (1.0 + jnp.exp(-gate)) * up

    for n in range(blocks):
        out_ref[n * half * lead : (n + 1) * half * lead, :] = act(
            n * wide * lead, half * lead
        ).astype(out_ref.dtype)
    others = [act(blocks * wide * lead + n * wide, half) for n in range(blocks * rest)]
    if others:
        out_ref[blocks * half * lead :, :] = jnp.concatenate(others, axis=0).astype(out_ref.dtype)


def activate_packed(parts, blocks, after):
    outs = [jax.ShapeDtypeStruct((parts[0].shape[0] // 2, 128), jnp.bfloat16)]
    return call(functools.partial(act_packed_kernel, blocks), "act", outs, parts, after)[0]


def down_packed_kernel(parts, blocks, *refs):
    acts, weights, outs, held = refs[:parts], refs[parts : parts + 2], refs[parts + 2 : -1], refs[-1]
    me = lax.axis_index("fsdp")
    quarter = weights[0].shape[0] // parts
    total = None
    for k, act in enumerate(acts):
        at = k * 2 * quarter
        unpack([(act, blocks)], held, at)
        depth = pl.ds(pl.multiple_of((me ^ k) * quarter, quarter), quarter)
        for j, w in enumerate(weights):
            term = jnp.dot(
                held[:, at + j * quarter : at + (j + 1) * quarter],
                w[depth, :],
                preferred_element_type=jnp.float32,
            )
            total = term if total is None else total + term
    for n, out in enumerate(outs):
        pack(out, total, 1, n, blocks)


def down_packed(acts, weights, blocks, after):
    depth, width = weights[0].shape
    rows = room_for(blocks)
    outs = [jax.ShapeDtypeStruct((packed_rows(1, width), 128), jnp.bfloat16)] * blocks
    kernel = functools.partial(down_packed_kernel, len(acts), blocks)
    flops = 4 * rows * depth * width
    scratch = [pltpu.VMEM((rows, 2 * depth), acts[0].dtype)]
    return call(kernel, "down", outs, [*acts, *weights], after, flops, scratch)


def combine_packed_kernel(back_high, back_low, *refs):
    terms, out_ref, held = refs[:-2], refs[-2], refs[-1]
    lead, rest = lead_of(CAP)
    total = terms[0][...].astype(jnp.float32)
    for term in terms[1:]:
        total += term[...].astype(jnp.float32)
    wide = total.shape[0] // CAP
    others = [jnp.zeros((held.shape[0] - CAP, 128 * wide), jnp.float32)]
    for n in range(rest):
        start = wide * lead + n * wide
        rows = [total[start + j : start + j + 1] for j in range(wide)]
        others.insert(n, jnp.concatenate(rows, axis=1))
    for j in range(wide):
        held[:lead, 128 * j : 128 * (j + 1)] = total[j * lead : (j + 1) * lead]
    held[lead:, :] = jnp.concatenate(others, axis=0)
    high, low = split(held[...])
    total = jnp.dot(back_low[...], high, preferred_element_type=jnp.float32)
    total += jnp.dot(back_high[...], low, preferred_element_type=jnp.float32)
    total += jnp.dot(back_high[...], high, preferred_element_type=jnp.float32)
    out_ref[...] = total.astype(out_ref.dtype)


def combine_packed(backs, terms):
    tokens, slots = backs[0].shape
    width = terms[0].shape[0] // CAP * 128
    outs = [jax.ShapeDtypeStruct((tokens, width), jnp.bfloat16)]
    scratch = [pltpu.VMEM((slots, width), jnp.float32)]
    return call(combine_packed_kernel, "combine", outs, [*backs, *terms], scratch=scratch)[0]


def local(n_fsdp, n_ed, groups, zorder, seq, tokens, expert_ids, route_weights, w_gate, w_up, w_down):
    slots = -(-CAP // 8) * 8
    swap = lambda v, axis, size, k: lax.ppermute(v, axis, [(i, i ^ k) for i in range(size)])
    partner = lambda v: swap(v, "ed", n_ed, 1)
    along = lambda v, s: swap(v, "ed", n_ed, 2 * s)
    across = lambda v, k: swap(v, "fsdp", n_fsdp, k)
    packed = w_gate.shape[2] % (128 * n_fsdp) == 0 and tokens.shape[1] % 128 == 0

    own = [w_gate[0], w_up[0], w_down[0]]
    other = [partner(w) for w in own]
    mine = pick_packed(expert_ids.T, tokens) if packed else pick(expert_ids.T, tokens, slots)
    backs = back(expert_ids.T, route_weights.T, slots, (mine,))
    blocks = {0: mine}
    for s in zorder:
        blocks[s] = along(mine, s)

    parts, acts, terms, last = {}, {}, [], (backs[0],)
    for word in seq:
        op, g = word[0], int(word[1:])
        group = groups[g]
        if op == "P":
            xs = [blocks[s] for s in group]
            weights = [own[0], other[0], own[1], other[1]]
            deps = (*last, other[2]) if g == WAIT else last
            out = (project_packed if packed else project)(xs, weights, n_fsdp, deps)
            parts[g] = [out[0]] + [across(out[k], k) for k in range(n_fsdp - 1, 0, -1)][::-1]
            last = (out[0],)
        elif op == "A":
            act = activate_packed(parts[g], len(group), last) if packed else activate(parts[g], last)
            acts[g] = [act] + [across(act, k) for k in range(n_fsdp - 1, 0, -1)][::-1]
            last = (act,)
        else:
            outs = (down_packed if packed else down)(acts[g], [own[2], other[2]], len(group), last)
            last = (outs[0],)
            terms += [out if s == 0 else along(out, s) for s, out in zip(group, outs)]
    return (combine_packed if packed else combine)(backs, terms)


def plan(n_ed):
    if n_ed == 8:
        return GROUPS, ZORDER, SEQ
    half = n_ed // 4
    groups = (tuple(range(half)), tuple(range(half, n_ed // 2)))
    return groups, tuple(range(1, n_ed // 2)), ("P0", "P1", "A0", "A1", "D0", "D1")


def solution(mesh):
    n_fsdp, n_ed = mesh.shape["fsdp"], mesh.shape["ed"]
    return jax.shard_map(
        functools.partial(local, n_fsdp, n_ed, *plan(n_ed)),
        mesh=mesh,
        in_specs=(
            P("ed", "fsdp"),
            P("ed", None),
            P("ed", None),
            P(None, "fsdp", "ed"),
            P(None, "fsdp", "ed"),
            P(None, "ed", "fsdp"),
        ),
        out_specs=P("ed", "fsdp"),
        check_vma=False,
    )
```

```python
import functools
import jax
import jax.numpy as jnp
from jax import lax
from jax.experimental import pallas as pl
from jax.experimental.pallas import tpu as pltpu
from jax.sharding import PartitionSpec as P

CAP = 81
LIMIT = 8 * 1024 * 1024
GROUPS = ((0, 1), (3,), (2,))
SEQ = ("P0", "P1", "A0", "P2", "A1", "D1", "A2", "D0", "D2")
WAIT = 1
ZORDER = (1, 3, 2)


def call(kernel, name, outs, args, after=(), flops=0, scratch=()):
    def body(*refs):
        kernel(*refs[len(after) :])

    return pl.pallas_call(
        body,
        out_shape=outs,
        in_specs=[pl.BlockSpec(memory_space=pl.ANY)] * len(after)
        + [pl.BlockSpec(memory_space=pltpu.VMEM)] * len(args),
        out_specs=[pl.BlockSpec(memory_space=pltpu.VMEM)] * len(outs),
        scratch_shapes=list(scratch),
        compiler_params=pltpu.CompilerParams(vmem_limit_bytes=LIMIT),
        cost_estimate=pl.CostEstimate(flops=flops, bytes_accessed=0, transcendentals=0),
        name=name,
    )(*after, *args)


def slot_hits(ids, slots):
    tokens = ids.shape[1]
    routed = jnp.max(jnp.where(ids == 0, 1.0, 0.0), axis=0, keepdims=True)
    upto = lax.broadcasted_iota(jnp.int32, (tokens, tokens), 0) <= lax.broadcasted_iota(
        jnp.int32, (tokens, tokens), 1
    )
    place = jnp.dot(
        jnp.broadcast_to(routed, (8, tokens)).astype(jnp.bfloat16),
        jnp.where(upto, 1.0, 0.0).astype(jnp.bfloat16),
        preferred_element_type=jnp.float32,
    )[0:1]
    place = jnp.where(routed > 0, place, 0.0)
    numbers = lax.broadcasted_iota(jnp.int32, (slots, tokens), 0).astype(jnp.float32) + 1.0
    return jnp.where(numbers == place, 1.0, 0.0)


def pick_kernel(ids_ref, tokens_ref, out_ref):
    hits = slot_hits(ids_ref[...], out_ref.shape[0])
    out_ref[...] = jnp.dot(
        hits.astype(jnp.bfloat16), tokens_ref[...], preferred_element_type=jnp.float32
    ).astype(out_ref.dtype)


def pick(ids, tokens, slots):
    outs = [jax.ShapeDtypeStruct((slots, tokens.shape[1]), tokens.dtype)]
    return call(pick_kernel, "pick", outs, [ids, tokens], flops=30000000000)[0]


def split(value):
    high = value.astype(jnp.bfloat16)
    return high, (value - high.astype(jnp.float32)).astype(jnp.bfloat16)


def back_kernel(ids_ref, scales_ref, hits_ref, scale_ref):
    ids = ids_ref[...]
    scale = jnp.sum(jnp.where(ids == 0, scales_ref[...], 0.0), axis=0, keepdims=True)
    hits = slot_hits(ids, hits_ref.shape[1])
    hits_ref[...] = hits.T.astype(hits_ref.dtype)
    scale_ref[...] = jnp.broadcast_to(scale, (scale_ref.shape[1], scale.shape[1])).T


def back(ids, scales, slots, after):
    outs = [
        jax.ShapeDtypeStruct((ids.shape[1], slots), jnp.bfloat16),
        jax.ShapeDtypeStruct((ids.shape[1], 128), jnp.float32),
    ]
    return call(back_kernel, "back", outs, [ids, scales], after)


def project_kernel(parts, n_x, *refs):
    xs, weights, outs = refs[:n_x], refs[n_x:-parts], refs[-parts:]
    me = lax.axis_index("fsdp")
    x = xs[0][...] if n_x == 1 else jnp.concatenate([r[...] for r in xs], axis=0)
    quarter = weights[0].shape[1] // parts
    for k in [*range(parts - 1, 0, -1), 0]:
        cols = pl.ds(pl.multiple_of((me ^ k) * quarter, quarter), quarter)
        for j, w in enumerate(weights):
            outs[k][:, j * quarter : (j + 1) * quarter] = jnp.dot(
                x, w[:, cols], preferred_element_type=jnp.float32
            ).astype(outs[k].dtype)


def project(xs, weights, parts, after):
    rows, depth = len(xs) * xs[0].shape[0], xs[0].shape[1]
    quarter = weights[0].shape[1] // parts
    kinds = [jnp.float32] + [jnp.bfloat16] * (parts - 1)
    if quarter % 128:
        outs = []
        me = lax.axis_index("fsdp")
        x = jnp.concatenate(xs, axis=0)
        for k, kind in enumerate(kinds):
            cut = [
                lax.dynamic_slice_in_dim(w, (me ^ k) * quarter, quarter, axis=1) for w in weights
            ]
            out = jnp.dot(x, jnp.concatenate(cut, axis=1), preferred_element_type=jnp.float32)
            outs.append(out.astype(kind))
        return outs
    outs = [jax.ShapeDtypeStruct((rows, len(weights) * quarter), k) for k in kinds]
    kernel = functools.partial(project_kernel, parts, len(xs))
    flops = 2 * rows * depth * len(weights) * quarter * parts
    return call(kernel, "project", outs, [*xs, *weights], after, flops)


def act_kernel(*refs):
    parts, out_ref = refs[:-1], refs[-1]
    total = parts[0][...]
    for part in parts[1:]:
        total += part[...].astype(jnp.float32)
    half = total.shape[1] // 2
    gate, up = total[:, :half], total[:, half:]
    out_ref[...] = (gate / (1.0 + jnp.exp(-gate)) * up).astype(out_ref.dtype)


def activate(parts, after):
    rows, width = parts[0].shape
    outs = [jax.ShapeDtypeStruct((rows, width // 2), jnp.bfloat16)]
    return call(act_kernel, "act", outs, parts, after)[0]


def down_kernel(parts, n_w, *refs):
    acts, weights, outs = refs[:parts], refs[parts : parts + n_w], refs[parts + n_w :]
    me = lax.axis_index("fsdp")
    quarter = weights[0].shape[0] // parts
    rows = outs[0].shape[0]
    total = None
    for k, act in enumerate(acts):
        depth = pl.ds(pl.multiple_of((me ^ k) * quarter, quarter), quarter)
        for j, w in enumerate(weights):
            term = jnp.dot(
                act[:, j * quarter : (j + 1) * quarter],
                w[depth, :],
                preferred_element_type=jnp.float32,
            )
            total = term if total is None else total + term
    for i, out in enumerate(outs):
        out[...] = total[i * rows : (i + 1) * rows].astype(out.dtype)


def down(acts, weights, blocks, after):
    parts, rows, width = len(acts), acts[0].shape[0], weights[0].shape[1]
    outs = [jax.ShapeDtypeStruct((rows // blocks, width), jnp.bfloat16)] * blocks
    kernel = functools.partial(down_kernel, parts, len(weights))
    flops = 2 * rows * weights[0].shape[0] * len(weights) * width
    return call(kernel, "down", outs, [*acts, *weights], after, flops)


def combine_kernel(hits, scale, *refs):
    terms, out_ref = refs[:-1], refs[-1]
    slot_out = terms[0][...].astype(jnp.float32)
    for term in terms[1:]:
        slot_out += term[...].astype(jnp.float32)
    high, low = split(slot_out)
    total = jnp.dot(hits[...], low, preferred_element_type=jnp.float32)
    total += jnp.dot(hits[...], high, preferred_element_type=jnp.float32)
    out_ref[...] = (total * scale[:, 0:1]).astype(out_ref.dtype)


def combine(backs, terms):
    outs = [jax.ShapeDtypeStruct((backs[0].shape[0], terms[0].shape[1]), jnp.bfloat16)]
    return call(combine_kernel, "combine", outs, [*backs, *terms])[0]


def lead_of(count):
    lead = count // 16 * 16
    return lead, count - lead


def packed_rows(blocks, columns):
    return blocks * CAP * columns // 128


def to_rows(value):
    return [value[:, 128 * j : 128 * (j + 1)] for j in range(value.shape[1] // 128)]


def pack(out_ref, value, blocks, first=0, of=None):
    lead, rest = lead_of(CAP)
    of = blocks if of is None else of
    wide = value.shape[1] // 128
    for n in range(blocks):
        for j in range(wide):
            out_ref[(n * wide + j) * lead : (n * wide + j + 1) * lead, :] = value[
                (first + n) * lead : (first + n + 1) * lead, 128 * j : 128 * (j + 1)
            ].astype(out_ref.dtype)
    others = []
    for n in range(blocks):
        for i in range(rest):
            row = of * lead + (first + n) * rest + i
            others += to_rows(value[row : row + 1])
    if others:
        start = blocks * wide * lead
        out_ref[start : start + len(others), :] = jnp.concatenate(others, axis=0).astype(out_ref.dtype)


def unpack(refs, held, at=0):
    lead, rest = lead_of(CAP)
    blocks = sum(n for _, n in refs)
    others, done = [], 0
    for ref, count in refs:
        wide = ref.shape[0] // (count * CAP)
        for n in range(count):
            for j in range(wide):
                held[
                    (done + n) * lead : (done + n + 1) * lead, at + 128 * j : at + 128 * (j + 1)
                ] = ref[(n * wide + j) * lead : (n * wide + j + 1) * lead, :]
        if rest:
            last = ref[count * wide * lead : count * wide * (lead + rest), :].astype(jnp.float32)
            for n in range(count * rest):
                rows = [last[n * wide + j : n * wide + j + 1] for j in range(wide)]
                others.append(jnp.concatenate(rows, axis=1))
        done += count
    room = held.shape[0] - blocks * lead
    if room:
        width = 128 * wide
        others.append(jnp.zeros((room - len(others), width), jnp.float32))
        held[blocks * lead :, at : at + width] = jnp.concatenate(others, axis=0).astype(held.dtype)


def room_for(blocks):
    lead, rest = lead_of(CAP)
    return blocks * lead + -(-blocks * rest // 16) * 16


def pick_packed_kernel(ids_ref, tokens_ref, out_ref):
    hits = slot_hits(ids_ref[...], -(-CAP // 8) * 8).astype(jnp.bfloat16)
    pack(out_ref, jnp.dot(hits, tokens_ref[...], preferred_element_type=jnp.float32), 1)


def pick_packed(ids, tokens):
    outs = [jax.ShapeDtypeStruct((packed_rows(1, tokens.shape[1]), 128), tokens.dtype)]
    return call(pick_packed_kernel, "pick", outs, [ids, tokens], flops=30000000000)[0]


def project_packed_kernel(parts, chosen, n_x, *refs):
    xs, weights, outs, held = refs[:n_x], refs[n_x : n_x + 4], refs[n_x + 4 : -1], refs[-1]
    me = lax.axis_index("fsdp")
    unpack([(x, 1) for x in xs], held)
    x = held[...]
    quarter = weights[0].shape[1] // parts
    for out, k in zip(outs, chosen):
        cols = pl.ds(pl.multiple_of((me ^ k) * quarter, quarter), quarter)
        value = [jnp.dot(x, w[:, cols], preferred_element_type=jnp.float32) for w in weights]
        pack(out, jnp.concatenate(value, axis=1), n_x)


def project_packed(xs, weights, parts, chosen, after):
    depth, width = weights[0].shape
    quarter = width // parts
    rows = room_for(len(xs))
    kinds = [jnp.bfloat16 if k else jnp.float32 for k in chosen]
    size = (packed_rows(len(xs), len(weights) * quarter), 128)
    outs = [jax.ShapeDtypeStruct(size, kind) for kind in kinds]
    kernel = functools.partial(project_packed_kernel, parts, chosen, len(xs))
    flops = 2 * rows * depth * len(weights) * quarter * len(chosen)
    scratch = [pltpu.VMEM((rows, depth), xs[0].dtype)]
    return call(kernel, "project", outs, [*xs, *weights], after, flops, scratch)


def act_packed_kernel(blocks, *refs):
    parts, out_ref = refs[:-1], refs[-1]
    total = parts[0][...]
    for part in parts[1:]:
        total += part[...].astype(jnp.float32)
    lead, rest = lead_of(CAP)
    wide = total.shape[0] // (blocks * CAP)
    half = wide // 2

    def act(start, rows):
        gate, up = total[start : start + rows], total[start + rows : start + 2 * rows]
        return gate / (1.0 + jnp.exp(-gate)) * up

    for n in range(blocks):
        out_ref[n * half * lead : (n + 1) * half * lead, :] = act(
            n * wide * lead, half * lead
        ).astype(out_ref.dtype)
    others = [act(blocks * wide * lead + n * wide, half) for n in range(blocks * rest)]
    if others:
        out_ref[blocks * half * lead :, :] = jnp.concatenate(others, axis=0).astype(out_ref.dtype)


def activate_packed(parts, blocks, after):
    outs = [jax.ShapeDtypeStruct((parts[0].shape[0] // 2, 128), jnp.bfloat16)]
    return call(functools.partial(act_packed_kernel, blocks), "act", outs, parts, after)[0]


def down_packed_kernel(parts, blocks, *refs):
    acts, weights, outs, held = refs[:parts], refs[parts : parts + 2], refs[parts + 2 : -1], refs[-1]
    me = lax.axis_index("fsdp")
    quarter = weights[0].shape[0] // parts
    total = None
    for k, act in enumerate(acts):
        at = k * 2 * quarter
        unpack([(act, blocks)], held, at)
        depth = pl.ds(pl.multiple_of((me ^ k) * quarter, quarter), quarter)
        for j, w in enumerate(weights):
            term = jnp.dot(
                held[:, at + j * quarter : at + (j + 1) * quarter],
                w[depth, :],
                preferred_element_type=jnp.float32,
            )
            total = term if total is None else total + term
    for n, out in enumerate(outs):
        pack(out, total, 1, n, blocks)


def down_packed(acts, weights, blocks, after):
    depth, width = weights[0].shape
    rows = room_for(blocks)
    outs = [jax.ShapeDtypeStruct((packed_rows(1, width), 128), jnp.bfloat16)] * blocks
    kernel = functools.partial(down_packed_kernel, len(acts), blocks)
    flops = 4 * rows * depth * width
    scratch = [pltpu.VMEM((rows, 2 * depth), acts[0].dtype)]
    return call(kernel, "down", outs, [*acts, *weights], after, flops, scratch)


def combine_packed_kernel(hits, scale, *refs):
    terms, out_ref, held = refs[:-2], refs[-2], refs[-1]
    lead, rest = lead_of(CAP)
    total = terms[0][...].astype(jnp.float32)
    for term in terms[1:]:
        total += term[...].astype(jnp.float32)
    wide = total.shape[0] // CAP
    others = [jnp.zeros((held.shape[0] - CAP, 128 * wide), jnp.float32)]
    for n in range(rest):
        start = wide * lead + n * wide
        rows = [total[start + j : start + j + 1] for j in range(wide)]
        others.insert(n, jnp.concatenate(rows, axis=1))
    for j in range(wide):
        held[:lead, 128 * j : 128 * (j + 1)] = total[j * lead : (j + 1) * lead]
    held[lead:, :] = jnp.concatenate(others, axis=0)
    high, low = split(held[...])
    total = jnp.dot(hits[...], low, preferred_element_type=jnp.float32)
    total += jnp.dot(hits[...], high, preferred_element_type=jnp.float32)
    out_ref[...] = (total * scale[:, 0:1]).astype(out_ref.dtype)


def combine_packed(backs, terms):
    tokens, slots = backs[0].shape
    width = terms[0].shape[0] // CAP * 128
    outs = [jax.ShapeDtypeStruct((tokens, width), jnp.bfloat16)]
    scratch = [pltpu.VMEM((slots, width), jnp.float32)]
    return call(combine_packed_kernel, "combine", outs, [*backs, *terms], scratch=scratch)[0]


def local(n_fsdp, n_ed, groups, zorder, seq, tokens, expert_ids, route_weights, w_gate, w_up, w_down):
    slots = -(-CAP // 8) * 8
    swap = lambda v, axis, size, k: lax.ppermute(v, axis, [(i, i ^ k) for i in range(size)])
    partner = lambda v: swap(v, "ed", n_ed, 1)
    along = lambda v, s: swap(v, "ed", n_ed, 2 * s)
    across = lambda v, k: swap(v, "fsdp", n_fsdp, k)
    packed = w_gate.shape[2] % (128 * n_fsdp) == 0 and tokens.shape[1] % 128 == 0

    own = [w_gate[0], w_up[0], w_down[0]]
    other = [partner(w) for w in own]
    mine = pick_packed(expert_ids.T, tokens) if packed else pick(expert_ids.T, tokens, slots)
    backs = back(expert_ids.T, route_weights.T, slots, (mine,))
    blocks = {0: mine}
    for s in zorder:
        blocks[s] = along(mine, s)

    parts, acts, terms, last = {}, {}, [], (backs[0],)
    for word in seq:
        op, g = word[0], int(word[1:])
        group = groups[g]
        if op == "P":
            xs = [blocks[s] for s in group]
            weights = [own[0], other[0], own[1], other[1]]
            deps = (*last, other[2]) if g == WAIT else last
            if packed:
                others = list(range(n_fsdp - 1, 0, -1))
                out = []
                for k in [*others, 0]:
                    out = [*project_packed(xs, weights, n_fsdp, [k], deps), *out]
                    deps = (out[0],)
            else:
                out = project(xs, weights, n_fsdp, deps)
            parts[g] = [out[0]] + [across(out[k], k) for k in range(n_fsdp - 1, 0, -1)][::-1]
            last = (out[0],)
        elif op == "A":
            act = activate_packed(parts[g], len(group), last) if packed else activate(parts[g], last)
            acts[g] = [act] + [across(act, k) for k in range(n_fsdp - 1, 0, -1)][::-1]
            last = (act,)
        else:
            outs = (down_packed if packed else down)(acts[g], [own[2], other[2]], len(group), last)
            last = (outs[0],)
            terms += [out if s == 0 else along(out, s) for s, out in zip(group, outs)]
    return (combine_packed if packed else combine)(backs, terms)


def plan(n_ed):
    if n_ed == 8:
        return GROUPS, ZORDER, SEQ
    half = n_ed // 4
    groups = (tuple(range(half)), tuple(range(half, n_ed // 2)))
    return groups, tuple(range(1, n_ed // 2)), ("P0", "P1", "A0", "A1", "D0", "D1")


def solution(mesh):
    n_fsdp, n_ed = mesh.shape["fsdp"], mesh.shape["ed"]
    return jax.shard_map(
        functools.partial(local, n_fsdp, n_ed, *plan(n_ed)),
        mesh=mesh,
        in_specs=(
            P("ed", "fsdp"),
            P("ed", None),
            P("ed", None),
            P(None, "fsdp", "ed"),
            P(None, "fsdp", "ed"),
            P(None, "ed", "fsdp"),
        ),
        out_specs=P("ed", "fsdp"),
        check_vma=False,
    )
```

```python
import functools
import jax
import jax.numpy as jnp
from jax import lax
from jax.experimental import pallas as pl
from jax.experimental.pallas import tpu as pltpu
from jax.sharding import PartitionSpec as P

CAP = 81
LIMIT = 8 * 1024 * 1024
GROUPS = ((0, 1), (3,), (2,))
SEQ = ("P0", "P1", "A0", "P2", "A1", "D1", "A2", "D0", "D2")
WAIT = 1
ZORDER = (1, 3, 2)


def call(kernel, name, outs, args, after=(), flops=0, scratch=()):
    def body(*refs):
        kernel(*refs[len(after) :])

    return pl.pallas_call(
        body,
        out_shape=outs,
        in_specs=[pl.BlockSpec(memory_space=pl.ANY)] * len(after)
        + [pl.BlockSpec(memory_space=pltpu.VMEM)] * len(args),
        out_specs=[pl.BlockSpec(memory_space=pltpu.VMEM)] * len(outs),
        scratch_shapes=list(scratch),
        compiler_params=pltpu.CompilerParams(vmem_limit_bytes=LIMIT),
        cost_estimate=pl.CostEstimate(flops=flops, bytes_accessed=0, transcendentals=0),
        name=name,
    )(*after, *args)


def slot_hits(ids, slots):
    tokens = ids.shape[1]
    routed = jnp.max(jnp.where(ids == 0, 1.0, 0.0), axis=0, keepdims=True)
    upto = lax.broadcasted_iota(jnp.int32, (tokens, tokens), 0) <= lax.broadcasted_iota(
        jnp.int32, (tokens, tokens), 1
    )
    place = jnp.dot(
        jnp.broadcast_to(routed, (8, tokens)).astype(jnp.bfloat16),
        jnp.where(upto, 1.0, 0.0).astype(jnp.bfloat16),
        preferred_element_type=jnp.float32,
    )[0:1]
    place = jnp.where(routed > 0, place, 0.0)
    numbers = lax.broadcasted_iota(jnp.int32, (slots, tokens), 0).astype(jnp.float32) + 1.0
    return jnp.where(numbers == place, 1.0, 0.0)


def pick_kernel(ids_ref, tokens_ref, out_ref):
    hits = slot_hits(ids_ref[...], out_ref.shape[0])
    out_ref[...] = jnp.dot(
        hits.astype(jnp.bfloat16), tokens_ref[...], preferred_element_type=jnp.float32
    ).astype(out_ref.dtype)


def pick(ids, tokens, slots):
    outs = [jax.ShapeDtypeStruct((slots, tokens.shape[1]), tokens.dtype)]
    return call(pick_kernel, "pick", outs, [ids, tokens], flops=30000000000)[0]


def split(value):
    high = value.astype(jnp.bfloat16)
    return high, (value - high.astype(jnp.float32)).astype(jnp.bfloat16)


def back_kernel(ids_ref, scales_ref, hits_ref, scale_ref):
    ids = ids_ref[...]
    scale = jnp.sum(jnp.where(ids == 0, scales_ref[...], 0.0), axis=0, keepdims=True)
    hits = slot_hits(ids, hits_ref.shape[1])
    hits_ref[...] = hits.T.astype(hits_ref.dtype)
    scale_ref[...] = jnp.broadcast_to(scale, (scale_ref.shape[1], scale.shape[1])).T


def back(ids, scales, slots, after):
    outs = [
        jax.ShapeDtypeStruct((ids.shape[1], slots), jnp.bfloat16),
        jax.ShapeDtypeStruct((ids.shape[1], 128), jnp.float32),
    ]
    return call(back_kernel, "back", outs, [ids, scales], after)


def project_kernel(parts, n_x, *refs):
    xs, weights, outs = refs[:n_x], refs[n_x:-parts], refs[-parts:]
    me = lax.axis_index("fsdp")
    x = xs[0][...] if n_x == 1 else jnp.concatenate([r[...] for r in xs], axis=0)
    quarter = weights[0].shape[1] // parts
    for k in [*range(parts - 1, 0, -1), 0]:
        cols = pl.ds(pl.multiple_of((me ^ k) * quarter, quarter), quarter)
        for j, w in enumerate(weights):
            outs[k][:, j * quarter : (j + 1) * quarter] = jnp.dot(
                x, w[:, cols], preferred_element_type=jnp.float32
            ).astype(outs[k].dtype)


def project(xs, weights, parts, after):
    rows, depth = len(xs) * xs[0].shape[0], xs[0].shape[1]
    quarter = weights[0].shape[1] // parts
    kinds = [jnp.float32] + [jnp.bfloat16] * (parts - 1)
    if quarter % 128:
        outs = []
        me = lax.axis_index("fsdp")
        x = jnp.concatenate(xs, axis=0)
        for k, kind in enumerate(kinds):
            cut = [
                lax.dynamic_slice_in_dim(w, (me ^ k) * quarter, quarter, axis=1) for w in weights
            ]
            out = jnp.dot(x, jnp.concatenate(cut, axis=1), preferred_element_type=jnp.float32)
            outs.append(out.astype(kind))
        return outs
    outs = [jax.ShapeDtypeStruct((rows, len(weights) * quarter), k) for k in kinds]
    kernel = functools.partial(project_kernel, parts, len(xs))
    flops = 2 * rows * depth * len(weights) * quarter * parts
    return call(kernel, "project", outs, [*xs, *weights], after, flops)


def act_kernel(*refs):
    parts, out_ref = refs[:-1], refs[-1]
    total = parts[0][...]
    for part in parts[1:]:
        total += part[...].astype(jnp.float32)
    half = total.shape[1] // 2
    gate, up = total[:, :half], total[:, half:]
    out_ref[...] = (gate / (1.0 + jnp.exp(-gate)) * up).astype(out_ref.dtype)


def activate(parts, after):
    rows, width = parts[0].shape
    outs = [jax.ShapeDtypeStruct((rows, width // 2), jnp.bfloat16)]
    return call(act_kernel, "act", outs, parts, after)[0]


def down_kernel(parts, n_w, *refs):
    acts, weights, outs = refs[:parts], refs[parts : parts + n_w], refs[parts + n_w :]
    me = lax.axis_index("fsdp")
    quarter = weights[0].shape[0] // parts
    rows = outs[0].shape[0]
    total = None
    for k, act in enumerate(acts):
        depth = pl.ds(pl.multiple_of((me ^ k) * quarter, quarter), quarter)
        for j, w in enumerate(weights):
            term = jnp.dot(
                act[:, j * quarter : (j + 1) * quarter],
                w[depth, :],
                preferred_element_type=jnp.float32,
            )
            total = term if total is None else total + term
    for i, out in enumerate(outs):
        out[...] = total[i * rows : (i + 1) * rows].astype(out.dtype)


def down(acts, weights, blocks, after):
    parts, rows, width = len(acts), acts[0].shape[0], weights[0].shape[1]
    outs = [jax.ShapeDtypeStruct((rows // blocks, width), jnp.bfloat16)] * blocks
    kernel = functools.partial(down_kernel, parts, len(weights))
    flops = 2 * rows * weights[0].shape[0] * len(weights) * width
    return call(kernel, "down", outs, [*acts, *weights], after, flops)


def combine_kernel(hits, scale, *refs):
    terms, out_ref = refs[:-1], refs[-1]
    slot_out = terms[0][...].astype(jnp.float32)
    for term in terms[1:]:
        slot_out += term[...].astype(jnp.float32)
    high, low = split(slot_out)
    total = jnp.dot(hits[...], low, preferred_element_type=jnp.float32)
    total += jnp.dot(hits[...], high, preferred_element_type=jnp.float32)
    out_ref[...] = (total * scale[:, 0:1]).astype(out_ref.dtype)


def combine(backs, terms):
    outs = [jax.ShapeDtypeStruct((backs[0].shape[0], terms[0].shape[1]), jnp.bfloat16)]
    return call(combine_kernel, "combine", outs, [*backs, *terms])[0]


def lead_of(count):
    lead = count // 16 * 16
    return lead, count - lead


def packed_rows(blocks, columns):
    return blocks * CAP * columns // 128


def to_rows(value):
    return [value[:, 128 * j : 128 * (j + 1)] for j in range(value.shape[1] // 128)]


def pack(out_ref, value, blocks, first=0, of=None):
    lead, rest = lead_of(CAP)
    of = blocks if of is None else of
    wide = value.shape[1] // 128
    for n in range(blocks):
        for j in range(wide):
            out_ref[(n * wide + j) * lead : (n * wide + j + 1) * lead, :] = value[
                (first + n) * lead : (first + n + 1) * lead, 128 * j : 128 * (j + 1)
            ].astype(out_ref.dtype)
    others = []
    for n in range(blocks):
        for i in range(rest):
            row = of * lead + (first + n) * rest + i
            others += to_rows(value[row : row + 1])
    if others:
        start = blocks * wide * lead
        out_ref[start : start + len(others), :] = jnp.concatenate(others, axis=0).astype(out_ref.dtype)


def unpack(refs, held, at=0):
    lead, rest = lead_of(CAP)
    blocks = sum(n for _, n in refs)
    others, done = [], 0
    for ref, count in refs:
        wide = ref.shape[0] // (count * CAP)
        for n in range(count):
            for j in range(wide):
                held[
                    (done + n) * lead : (done + n + 1) * lead, at + 128 * j : at + 128 * (j + 1)
                ] = ref[(n * wide + j) * lead : (n * wide + j + 1) * lead, :]
        if rest:
            last = ref[count * wide * lead : count * wide * (lead + rest), :].astype(jnp.float32)
            for n in range(count * rest):
                rows = [last[n * wide + j : n * wide + j + 1] for j in range(wide)]
                others.append(jnp.concatenate(rows, axis=1))
        done += count
    room = held.shape[0] - blocks * lead
    if room:
        width = 128 * wide
        others.append(jnp.zeros((room - len(others), width), jnp.float32))
        held[blocks * lead :, at : at + width] = jnp.concatenate(others, axis=0).astype(held.dtype)


def room_for(blocks):
    lead, rest = lead_of(CAP)
    return blocks * lead + -(-blocks * rest // 16) * 16


def pick_packed_kernel(ids_ref, tokens_ref, out_ref):
    hits = slot_hits(ids_ref[...], -(-CAP // 8) * 8).astype(jnp.bfloat16)
    pack(out_ref, jnp.dot(hits, tokens_ref[...], preferred_element_type=jnp.float32), 1)


def pick_packed(ids, tokens):
    outs = [jax.ShapeDtypeStruct((packed_rows(1, tokens.shape[1]), 128), tokens.dtype)]
    return call(pick_packed_kernel, "pick", outs, [ids, tokens], flops=30000000000)[0]


def project_packed_kernel(parts, chosen, n_x, *refs):
    xs, weights, outs, held = refs[:n_x], refs[n_x : n_x + 4], refs[n_x + 4 : -1], refs[-1]
    me = lax.axis_index("fsdp")
    unpack([(x, 1) for x in xs], held)
    x = held[...]
    quarter = weights[0].shape[1] // parts
    for out, k in zip(outs, chosen):
        cols = pl.ds(pl.multiple_of((me ^ k) * quarter, quarter), quarter)
        value = [jnp.dot(x, w[:, cols], preferred_element_type=jnp.float32) for w in weights]
        pack(out, jnp.concatenate(value, axis=1), n_x)


def project_packed(xs, weights, parts, chosen, after):
    depth, width = weights[0].shape
    quarter = width // parts
    rows = room_for(len(xs))
    kinds = [jnp.bfloat16 if k else jnp.float32 for k in chosen]
    size = (packed_rows(len(xs), len(weights) * quarter), 128)
    outs = [jax.ShapeDtypeStruct(size, kind) for kind in kinds]
    kernel = functools.partial(project_packed_kernel, parts, chosen, len(xs))
    flops = 2 * rows * depth * len(weights) * quarter * len(chosen)
    scratch = [pltpu.VMEM((rows, depth), xs[0].dtype)]
    return call(kernel, "project", outs, [*xs, *weights], after, flops, scratch)


def act_packed_kernel(blocks, *refs):
    parts, out_ref = refs[:-1], refs[-1]
    total = parts[0][...]
    for part in parts[1:]:
        total += part[...].astype(jnp.float32)
    lead, rest = lead_of(CAP)
    wide = total.shape[0] // (blocks * CAP)
    half = wide // 2

    def act(start, rows):
        gate, up = total[start : start + rows], total[start + rows : start + 2 * rows]
        return gate / (1.0 + jnp.exp(-gate)) * up

    for n in range(blocks):
        out_ref[n * half * lead : (n + 1) * half * lead, :] = act(
            n * wide * lead, half * lead
        ).astype(out_ref.dtype)
    others = [act(blocks * wide * lead + n * wide, half) for n in range(blocks * rest)]
    if others:
        out_ref[blocks * half * lead :, :] = jnp.concatenate(others, axis=0).astype(out_ref.dtype)


def activate_packed(parts, blocks, after):
    outs = [jax.ShapeDtypeStruct((parts[0].shape[0] // 2, 128), jnp.bfloat16)]
    return call(functools.partial(act_packed_kernel, blocks), "act", outs, parts, after)[0]


def down_packed_kernel(parts, blocks, *refs):
    acts, weights, outs, held = refs[:parts], refs[parts : parts + 2], refs[parts + 2 : -1], refs[-1]
    me = lax.axis_index("fsdp")
    quarter = weights[0].shape[0] // parts
    total = None
    for k, act in enumerate(acts):
        at = k * 2 * quarter
        unpack([(act, blocks)], held, at)
        depth = pl.ds(pl.multiple_of((me ^ k) * quarter, quarter), quarter)
        for j, w in enumerate(weights):
            term = jnp.dot(
                held[:, at + j * quarter : at + (j + 1) * quarter],
                w[depth, :],
                preferred_element_type=jnp.float32,
            )
            total = term if total is None else total + term
    for n, out in enumerate(outs):
        pack(out, total, 1, n, blocks)


def down_packed(acts, weights, blocks, after):
    depth, width = weights[0].shape
    rows = room_for(blocks)
    outs = [jax.ShapeDtypeStruct((packed_rows(1, width), 128), jnp.bfloat16)] * blocks
    kernel = functools.partial(down_packed_kernel, len(acts), blocks)
    flops = 4 * rows * depth * width
    scratch = [pltpu.VMEM((rows, 2 * depth), acts[0].dtype)]
    return call(kernel, "down", outs, [*acts, *weights], after, flops, scratch)


def combine_packed_kernel(hits, scale, *refs):
    terms, out_ref, held = refs[:-2], refs[-2], refs[-1]
    lead, rest = lead_of(CAP)
    total = terms[0][...].astype(jnp.float32)
    for term in terms[1:]:
        total += term[...].astype(jnp.float32)
    wide = total.shape[0] // CAP
    others = [jnp.zeros((held.shape[0] - CAP, 128 * wide), jnp.float32)]
    for n in range(rest):
        start = wide * lead + n * wide
        rows = [total[start + j : start + j + 1] for j in range(wide)]
        others.insert(n, jnp.concatenate(rows, axis=1))
    for j in range(wide):
        held[:lead, 128 * j : 128 * (j + 1)] = total[j * lead : (j + 1) * lead]
    held[lead:, :] = jnp.concatenate(others, axis=0)
    high, low = split(held[...])
    total = jnp.dot(hits[...], low, preferred_element_type=jnp.float32)
    total += jnp.dot(hits[...], high, preferred_element_type=jnp.float32)
    out_ref[...] = (total * scale[:, 0:1]).astype(out_ref.dtype)


def combine_packed(backs, terms):
    tokens, slots = backs[0].shape
    width = terms[0].shape[0] // CAP * 128
    outs = [jax.ShapeDtypeStruct((tokens, width), jnp.bfloat16)]
    scratch = [pltpu.VMEM((slots, width), jnp.float32)]
    return call(combine_packed_kernel, "combine", outs, [*backs, *terms], scratch=scratch)[0]


def local(n_fsdp, n_ed, groups, zorder, seq, tokens, expert_ids, route_weights, w_gate, w_up, w_down):
    slots = -(-CAP // 8) * 8
    swap = lambda v, axis, size, k: lax.ppermute(v, axis, [(i, i ^ k) for i in range(size)])
    partner = lambda v: swap(v, "ed", n_ed, 1)
    along = lambda v, s: swap(v, "ed", n_ed, 2 * s)
    across = lambda v, k: swap(v, "fsdp", n_fsdp, k)
    packed = w_gate.shape[2] % (128 * n_fsdp) == 0 and tokens.shape[1] % 128 == 0

    own = [w_gate[0], w_up[0], w_down[0]]
    other = [partner(w) for w in own]
    mine = pick_packed(expert_ids.T, tokens) if packed else pick(expert_ids.T, tokens, slots)
    backs = back(expert_ids.T, route_weights.T, slots, (mine,))
    blocks = {0: mine}
    for s in zorder:
        blocks[s] = along(mine, s)

    parts, acts, terms, last = {}, {}, [], (backs[0],)
    for word in seq:
        op, g = word[0], int(word[1:])
        group = groups[g]
        if op == "P":
            xs = [blocks[s] for s in group]
            weights = [own[0], other[0], own[1], other[1]]
            deps = (*last, other[2]) if g == WAIT else last
            if packed:
                others = list(range(1, n_fsdp))
                out = []
                for k in [*others, 0]:
                    out.append(project_packed(xs, weights, n_fsdp, [k], deps)[0])
                    deps = (out[-1],)
                out = [out[-1], *out[:-1]]
            else:
                out = project(xs, weights, n_fsdp, deps)
            parts[g] = [out[0]] + [across(out[k], k) for k in range(n_fsdp - 1, 0, -1)][::-1]
            last = (out[0],)
        elif op == "A":
            act = activate_packed(parts[g], len(group), last) if packed else activate(parts[g], last)
            acts[g] = [act] + [across(act, k) for k in range(n_fsdp - 1, 0, -1)][::-1]
            last = (act,)
        else:
            outs = (down_packed if packed else down)(acts[g], [own[2], other[2]], len(group), last)
            last = (outs[0],)
            terms += [out if s == 0 else along(out, s) for s, out in zip(group, outs)]
    return (combine_packed if packed else combine)(backs, terms)


def plan(n_ed):
    if n_ed == 8:
        return GROUPS, ZORDER, SEQ
    half = n_ed // 4
    groups = (tuple(range(half)), tuple(range(half, n_ed // 2)))
    return groups, tuple(range(1, n_ed // 2)), ("P0", "P1", "A0", "A1", "D0", "D1")


def solution(mesh):
    n_fsdp, n_ed = mesh.shape["fsdp"], mesh.shape["ed"]
    return jax.shard_map(
        functools.partial(local, n_fsdp, n_ed, *plan(n_ed)),
        mesh=mesh,
        in_specs=(
            P("ed", "fsdp"),
            P("ed", None),
            P("ed", None),
            P(None, "fsdp", "ed"),
            P(None, "fsdp", "ed"),
            P(None, "ed", "fsdp"),
        ),
        out_specs=P("ed", "fsdp"),
        check_vma=False,
    )
```
